512 devices in a mesh: gx: 8 (over z), gy: 8 (over y_lo, core), gz: 8 (over y_hi, x).
Axes of the slice: x: 4, y: 8 (y_hi: 2, y_lo: 4; y = y_hi * 4 + y_lo), z: 8, core: 2. Of those that a mesh axis runs over, the one named last changes fastest.
Arguments:
- operator: bfloat16 [8, 8, 8, 1152, 1152], P('gx', 'gy', 'gz'), may hold values from -0.1875 to 0.1875
- lift: bfloat16 [8, 8, 8, 1152, 128], P('gx', 'gy', 'gz'), may hold values from -0.5 to 0.5
- source: bfloat16 [8, 8, 8, 128, 256], P('gx', 'gy', 'gz'), may hold values from -6 to 6
- traces_in: bfloat16 [8, 8, 8, 1152, 256], P('gx', 'gy', 'gz'), may hold values from -6 to 6
- depth: int32 [8], replicated, may hold values from 0 to 6
- direction: int32 [8], replicated, may hold values from 0 to 1
Outputs:
- traces_out: bfloat16 [8, 8, 8, 1152, 256], P('gx', 'gy', 'gz')
The draws below stay inside these ranges and needn't reach their ends.
All inputs are finite; a program needn't handle non-finite values.
Results may differ from the reference program's by a relative error of at most 0.008.
Values may be sent and summed in bfloat16 or wider, within the bound.
A program may use at most 64 MiB of HBM per device.

```python
import jax
import jax.numpy as jnp
from jax import lax

FACE = 384
ORDER = 1152
SRC = 128
NB = 8
RB = 32
RHS = 256
STEPS = 6
N_GX = 8
N_GY = 8
N_GZ = 8


def set_ends(array, stream_key, smallest, high):
    longest = array.shape.index(max(array.shape))
    spots = []
    for shift in (0, 1):
        where = [jax.random.randint(jax.random.fold_in(stream_key, axis), (), 0, length) for axis, length in enumerate(array.shape)]
        where[longest] = (where[longest] + shift) % array.shape[longest]
        spots.append(tuple(where))
    return array.at[spots[0]].set(smallest).at[spots[1]].set(high)


def shard_levels(stream_key, dims, cuts, low, high):
    gain, own = 1.0, jax.random.fold_in(stream_key, 6)
    for axis_at, shards_of in cuts:
        draws = jnp.exp(jax.random.uniform(jax.random.fold_in(own, axis_at), (shards_of,), jnp.float32, low / len(cuts), high / len(cuts)))
        gain = gain * jnp.repeat(draws, dims[axis_at] // shards_of).reshape([-1 if axis == axis_at else 1 for axis in range(len(dims))])
    return gain


def gaussian(own_key, shape, width, limit, shards=(), kind=jnp.bfloat16):
    values = width * jax.random.normal(own_key, shape, jnp.float32)
    if shards:
        values = values * shard_levels(own_key, shape, shards, -0.22, 0.18)
    return jnp.clip(values, -limit, limit).astype(kind)


def setup_inputs(seed: int = 0) -> dict:
    seeds = jax.random.split(jax.random.key(seed), 7)
    operator = gaussian(seeds[0], (N_GX, N_GY, N_GZ, ORDER, ORDER), ORDER ** -0.5, 0.1875, ((0, 8), (1, 8), (2, 8)))
    lift = gaussian(seeds[1], (N_GX, N_GY, N_GZ, ORDER, SRC), SRC ** -0.5, 0.5, ((0, 8), (1, 8), (2, 8)))
    source = gaussian(seeds[2], (N_GX, N_GY, N_GZ, SRC, RHS), 1.0, 6.0, ((0, 8), (1, 8), (2, 8)))
    traces_in = gaussian(seeds[3], (N_GX, N_GY, N_GZ, ORDER, RHS), 1.0, 6.0, ((0, 8), (1, 8), (2, 8)))
    depth = set_ends(jax.random.randint(seeds[4], (NB,), 0, STEPS + 1), jax.random.fold_in(seeds[4], 1), 0, STEPS).astype(jnp.int32)
    direction = set_ends(jax.random.randint(seeds[5], (NB,), 0, 2), jax.random.fold_in(seeds[5], 1), 0, 1).astype(jnp.int32)
    return {"operator": operator, "lift": lift, "source": source, "traces_in": traces_in, "depth": depth, "direction": direction}


def block_product(pair):
    return jnp.dot(pair[0], pair[1], preferred_element_type=jnp.float32)


def neighbour_face(face, axis, backward):
    widths = [(0, 0)] * face.ndim
    widths[axis] = (1, 1)
    padded = jnp.pad(face, widths)
    count = face.shape[axis]
    lower = lax.slice_in_dim(padded, 0, count, axis=axis)
    upper = lax.slice_in_dim(padded, 2, count + 2, axis=axis)
    return jnp.where(backward, upper, lower)


def reference(operator, lift, source, traces_in, depth, direction):
    grid = operator.shape[:3]
    blocks = grid[0] * grid[1] * grid[2]
    flat_ops = operator.reshape(blocks, ORDER, ORDER)
    lifted = lax.map(block_product, (lift.reshape(blocks, ORDER, SRC), source.reshape(blocks, SRC, RHS)))
    backward = jnp.repeat(direction == 1, RB)
    state = traces_in
    for step in range(STEPS):
        gate = jnp.repeat(depth <= step, RB).astype(jnp.float32)
        product = lax.map(block_product, (flat_ops, state.reshape(blocks, ORDER, RHS)))
        outgoing = (product + gate * lifted).astype(jnp.bfloat16).reshape(grid + (ORDER, RHS))
        faces = []
        for axis in range(3):
            face = outgoing[:, :, :, axis * FACE:(axis + 1) * FACE, :]
            faces.append(neighbour_face(face, axis, backward))
        state = jnp.concatenate(faces, axis=3)
    return state
```

```python
import functools

import jax
import jax.numpy as jnp
from jax import lax
from jax.experimental import pallas as pl
from jax.experimental.pallas import tpu as pltpu
from jax.sharding import PartitionSpec as P

MESH = pl.DeviceIdType.MESH
FACE = 384
ORDER = 1152
SRC = 128
NB = 8
RB = 32
RHS = NB * RB
STEPS = 6
N = 8
CHUNKS = 2
LAG = 1
UP, DOWN = 0, 1
AXES = ("gx", "gy", "gz")
F32, BF16 = jnp.float32, jnp.bfloat16
NT = (((1,), (1,)), ((), ()))


def plan(n_up):
    ups = [n_up // CHUNKS + (c < n_up % CHUNKS) for c in range(CHUNKS)]
    n_down = NB - n_up
    downs = [n_down // CHUNKS + (CHUNKS - 1 - c < n_down % CHUNKS) for c in range(CHUNKS)]
    rows, place, at = [], {}, 0
    seen = [0, n_up]
    for c in range(CHUNKS):
        spans = []
        for kind, count in ((UP, ups[c]), (DOWN, downs[c])):
            spans.append((at, count * RB))
            for _ in range(count):
                place[seen[kind]] = at
                seen[kind] += 1
                at += RB
        rows.append(tuple(spans))
    return rows, place


def kernel(n_up, op_h, lift_h, src_h, tr_h, info_h, out, a, at, lf, sr, tr, st, og, lifted, hop, info, order, since,
           lsem, ssem, rsem, hsem, fsem):
    rows, place = plan(n_up)
    pos = [lax.axis_index(name) for name in AXES]
    gy, gz = pos[1], pos[2]
    odd = lax.rem(gy, 2) == 1
    high = (gz >= N // 2).astype(jnp.int32)
    ends = (gz == 3) | (gz == 4)
    ring = odd & (ends | (gz == 0) | (gz == N - 1))

    loads = [
        pltpu.make_async_copy(s, d, lsem.at[n])
        for n, (s, d) in enumerate(
            ((info_h, info), (tr_h, tr), (src_h, sr), (lift_h, lf), (op_h, a))
        )
    ]
    for load in loads:
        load.start()

    def direct(f, d):
        there = (pos[f] < N - 1) if d == UP else (pos[f] > 0)
        if f == 2:
            there &= jnp.logical_not(odd & (gz == (3 if d == UP else 4)))
        return there

    def step_to(f, d):
        return {AXES[f]: pos[f] + (1 if d == UP else -1)}

    barrier = pltpu.get_barrier_semaphore()
    peers = jnp.int32(0)
    for f in range(3):
        for d in (UP, DOWN):
            there = direct(f, d)
            peers += there.astype(jnp.int32)

            @pl.when(there)
            def _():
                pl.semaphore_signal(barrier, inc=1, device_id=step_to(f, d), device_id_type=MESH)

    peers += 2 * ring.astype(jnp.int32)
    for other in (jnp.where(ends, 0, 3), jnp.where(ends, N - 1, 4)):

        @pl.when(ring)
        def _():
            pl.semaphore_signal(barrier, inc=1, device_id={"gz": other}, device_id_type=MESH)

    for f in range(3):
        for d in (UP, DOWN):

            @pl.when(pos[f] == (0 if d == UP else N - 1))
            def _():
                for c in range(CHUNKS):
                    r0, nr = rows[c][d]
                    if nr:
                        for t in range(1, STEPS + 1):
                            st[t, r0 : r0 + nr, f * FACE : (f + 1) * FACE] = jnp.zeros((nr, FACE), BF16)

    loads[0].wait()

    def per_column(at_row):
        each = [jnp.broadcast_to(info[at_row + b : at_row + b + 1, :], (RB, 128)) for b in range(NB)]
        return jnp.concatenate(each, axis=0).astype(BF16)

    pick = jnp.where(lax.broadcasted_iota(jnp.int32, (16, 128), 1) == 0, 1.0, 0.0).astype(BF16)
    back = lax.dot_general(pick, per_column(0), NT, preferred_element_type=F32)
    rows_i = lax.broadcasted_iota(jnp.int32, (RHS, RHS), 0)
    cols_i = lax.broadcasted_iota(jnp.int32, (RHS, RHS), 1)
    before = jnp.where((rows_i >> 5) < (cols_i >> 5), 1.0, 0.0).astype(BF16)
    downs = jnp.dot(back.astype(BF16), before, preferred_element_type=F32) * (1.0 / RB)
    col = lax.broadcasted_iota(jnp.int32, (16, RHS), 1)
    key = jnp.where(back > 0.5, n_up + downs, (col >> 5).astype(F32) - downs)
    row_of = (col & (RB - 1)).astype(F32)
    for s in range(NB):
        row_of += jnp.where(key == s, float(place[s]), 0.0)
    order[...] = jnp.where(rows_i.astype(F32) == row_of[0:1, :], 1.0, 0.0).astype(BF16)
    since[...] = jnp.dot(order[...], per_column(NB), preferred_element_type=F32)
    unit = lax.broadcasted_iota(jnp.int32, (FACE, FACE), 0) == lax.broadcasted_iota(jnp.int32, (FACE, FACE), 1)
    unit = jnp.where(unit, 1.0, 0.0).astype(BF16)

    def span(f):
        return pl.ds(pl.multiple_of(f * FACE, FACE), FACE)

    loads[1].wait()
    loads[2].wait()
    loads[3].wait()
    coeffs = lax.dot_general(order[...], sr[...], NT, preferred_element_type=F32).astype(BF16)

    def begin(f, carry):
        st[0, :, span(f)] = lax.dot_general(order[...], tr[span(f), :], NT, preferred_element_type=F32).astype(BF16)
        lifted[:, span(f)] = lax.dot_general(coeffs, lf[span(f), :], NT, preferred_element_type=F32)
        return carry

    lax.fori_loop(0, 3, begin, 0)
    loads[4].wait()

    def flip(n, carry):
        k, f = n // 3, lax.rem(n, 3)
        at[span(k), span(f)] = lax.dot_general(unit, a[span(f), span(k)], NT, preferred_element_type=F32).astype(BF16)
        return carry

    lax.fori_loop(0, 9, flip, 0)

    def part(ref, t, c, d, f):
        r0, nr = rows[c][d]
        return ref.at[t, pl.ds(r0, nr), pl.ds(f * FACE, FACE)]

    def hop_part(t, c, d):
        r0, nr = rows[c][d]
        return hop.at[t, pl.ds(r0, nr), :]

    def send(t, c, d, f):
        return pltpu.make_async_remote_copy(
            src_ref=part(og, t, c, d, f), dst_ref=part(st, t + 1, c, d, f),
            send_sem=ssem.at[t, c, d, f], recv_sem=rsem.at[t, c, d, f],
            device_id=step_to(f, d), device_id_type=MESH,
        )

    def send_hop(t, c, d):
        return pltpu.make_async_remote_copy(
            src_ref=part(og, t, c, d, 2), dst_ref=hop_part(t, c, d),
            send_sem=ssem.at[t, c, d, 2], recv_sem=hsem.at[t, c],
            device_id={"gz": 0 if d == UP else N - 1}, device_id_type=MESH,
        )

    def send_on(t, c, d):
        return pltpu.make_async_remote_copy(
            src_ref=hop_part(t, c, d), dst_ref=part(st, t + 1, c, d, 2),
            send_sem=fsem.at[t, c], recv_sem=rsem.at[t, c, d, 2],
            device_id={"gz": 4 if d == UP else 3}, device_id_type=MESH,
        )

    def times(tau):
        return (tau - LAG * high, tau - LAG * (1 - high))

    def inside(t):
        return (t >= 0) & (t < STEPS)

    def arrive(t, c, d, last=STEPS - 1):
        if not rows[c][d][1]:
            return
        for f in (2, 0, 1):
            has = (pos[f] > 0) if d == UP else (pos[f] < N - 1)

            @pl.when(has & (t >= 1) & (t <= last))
            def _():
                send(t - 1, c, d, f).wait_recv()

    def sent(tau):
        for c in range(CHUNKS):
            for d, t in zip((UP, DOWN), times(tau)):
                if not rows[c][d][1]:
                    continue
                for f in range(3):
                    has = (pos[f] < N - 1) if d == UP else (pos[f] > 0)

                    @pl.when(has & inside(t - 1))
                    def _():
                        send(t - 1, c, d, f).wait_send()

                @pl.when(odd & (gz == (0 if d == UP else N - 1)) & inside(tau - 2))
                def _():
                    send_on(tau - 2, c, d).wait_send()

    def tick(tau, carry):
        ts = times(tau)
        read = [jnp.clip(t, 0, STEPS - 1) for t in ts]
        write = [jnp.clip(t, 0, STEPS) for t in ts]
        for c in range(CHUNKS):
            kinds = [d for d in (UP, DOWN) if rows[c][d][1]]
            for d in kinds:
                arrive(ts[d], c, d)

            def face(n, carry):
                f = lax.rem(n + 2, 3)
                x = jnp.concatenate([st[read[d], rows[c][d][0] : sum(rows[c][d]), :] for d in kinds], axis=0)
                acc = jnp.dot(x, at[:, span(f)], preferred_element_type=F32)
                at_row = 0
                for d in kinds:
                    r0, nr = rows[c][d]
                    gate = jnp.where(since[r0 : r0 + nr, :] <= ts[d].astype(F32), 1.0, 0.0)
                    gate = jnp.concatenate([gate] * (FACE // 128), axis=1)
                    total = acc[at_row : at_row + nr] + gate * lifted[r0 : r0 + nr, span(f)]
                    og[write[d], r0 : r0 + nr, span(f)] = total.astype(BF16)
                    at_row += nr
                for d in kinds:
                    for g in range(3):

                        @pl.when((f == g) & direct(g, d) & inside(ts[d]))
                        def _():
                            send(ts[d], c, d, g).start()

                    @pl.when((f == 2) & odd & (gz == (3 if d == UP else 4)) & inside(ts[d]))
                    def _():
                        send_hop(ts[d], c, d).start()

                return carry

            lax.fori_loop(0, 3, face, 0)
            for d in kinds:

                @pl.when(odd & (gz == (0 if d == UP else N - 1)) & inside(tau - 1))
                def _():
                    send_hop(tau - 1, c, d).wait_recv()
                    send_on(tau - 1, c, d).start()

        sent(tau)
        return carry

    pl.semaphore_wait(barrier, peers)
    lax.fori_loop(0, STEPS + LAG, tick, 0)
    sent(jnp.int32(STEPS + LAG))
    for c in range(CHUNKS):
        for d in (UP, DOWN):
            arrive(jnp.int32(STEPS), c, d, STEPS)

    def finish(f, carry):
        block = lax.dot_general(unit, st[STEPS, :, span(f)], NT, preferred_element_type=F32).astype(BF16)
        out[span(f), :] = jnp.dot(block, order[...], preferred_element_type=F32).astype(BF16)
        return carry

    lax.fori_loop(0, 3, finish, 0)


def sweep(n_up, operator, lift, source, traces_in, info, *_):
    anywhere = pl.BlockSpec(memory_space=pl.ANY)
    return pl.pallas_call(
        functools.partial(kernel, n_up),
        out_shape=jax.ShapeDtypeStruct((ORDER, RHS), BF16),
        in_specs=[anywhere] * 5,
        out_specs=pl.BlockSpec(memory_space=pltpu.VMEM),
        scratch_shapes=[
            pltpu.VMEM((ORDER, ORDER), BF16),
            pltpu.VMEM((ORDER, ORDER), BF16),
            pltpu.VMEM((ORDER, SRC), BF16),
            pltpu.VMEM((SRC, RHS), BF16),
            pltpu.VMEM((ORDER, RHS), BF16),
            pltpu.VMEM((STEPS + 1, RHS, ORDER), BF16),
            pltpu.VMEM((STEPS + 1, RHS, ORDER), BF16),
            pltpu.VMEM((RHS, ORDER), F32),
            pltpu.VMEM((STEPS, RHS, FACE), BF16),
            pltpu.VMEM((16, 128), F32),
            pltpu.VMEM((RHS, RHS), BF16),
            pltpu.VMEM((RHS, 128), F32),
            pltpu.SemaphoreType.DMA((5,)),
            pltpu.SemaphoreType.DMA((STEPS, CHUNKS, 2, 3)),
            pltpu.SemaphoreType.DMA((STEPS, CHUNKS, 2, 3)),
            pltpu.SemaphoreType.DMA((STEPS, CHUNKS)),
            pltpu.SemaphoreType.DMA((STEPS, CHUNKS)),
        ],
        compiler_params=pltpu.CompilerParams(
            collective_id=n_up, has_side_effects=True, vmem_limit_bytes=40 * 2**20
        ),
        name=f"sweep_{n_up}",
    )(operator, lift, source, traces_in, info)


VARIANTS = (3, 4, 5)


def general(operator, lift, source, traces_in, info, depth, direction):
    lifted = jnp.dot(lift, source, preferred_element_type=F32)
    backward = jnp.repeat(direction == 1, RB)
    level = jnp.repeat(depth, RB)
    up = [(i, i + 1) for i in range(N - 1)]
    down = [(i + 1, i) for i in range(N - 1)]

    def step(t, state):
        gate = (level <= t).astype(F32)
        outgoing = (jnp.dot(operator, state, preferred_element_type=F32) + gate * lifted).astype(BF16)
        faces = []
        for f, axis in enumerate(AXES):
            face = outgoing[f * FACE : (f + 1) * FACE]
            faces.append(jnp.where(backward, lax.ppermute(face, axis, down), lax.ppermute(face, axis, up)))
        return jnp.concatenate(faces, axis=0)

    return lax.fori_loop(0, STEPS, step, traces_in)


def body(operator, lift, source, traces_in, depth, direction):
    info = jnp.broadcast_to(jnp.concatenate([direction, depth]).astype(F32)[:, None], (2 * NB, 128))
    args = (operator[0, 0, 0], lift[0, 0, 0], source[0, 0, 0], traces_in[0, 0, 0], info, depth, direction)
    n_up = NB - jnp.sum((direction == 1).astype(jnp.int32))
    which = len(VARIANTS) + sum(jnp.where(n_up == n, i - len(VARIANTS), 0) for i, n in enumerate(VARIANTS))
    branches = [functools.partial(sweep, n) for n in VARIANTS] + [general]
    result = lax.switch(which, branches, *args)
    return result[None, None, None]


def solution(mesh):
    placed = (
        P("gx", "gy", "gz", None, None),
        P("gx", "gy", "gz", None, None),
        P("gx", "gy", "gz", None, None),
        P("gx", "gy", "gz", None, None),
        P(),
        P(),
    )
    return jax.shard_map(
        body, mesh=mesh, in_specs=placed, out_specs=P("gx", "gy", "gz", None, None), check_vma=False
    )
```

```python
import functools

import jax
import jax.numpy as jnp
from jax import lax
from jax.experimental import pallas as pl
from jax.experimental.pallas import tpu as pltpu
from jax.sharding import PartitionSpec as P

MESH = pl.DeviceIdType.MESH
FACE = 384
ORDER = 1152
SRC = 128
NB = 8
RB = 32
RHS = NB * RB
STEPS = 6
N = 8
CHUNKS = 2
LAG = 1
UP, DOWN = 0, 1
AXES = ("gx", "gy", "gz")
F32, BF16 = jnp.float32, jnp.bfloat16
NT = (((1,), (1,)), ((), ()))


def plan(n_up):
    ups = [n_up // CHUNKS + (c < n_up % CHUNKS) for c in range(CHUNKS)]
    n_down = NB - n_up
    downs = [n_down // CHUNKS + (CHUNKS - 1 - c < n_down % CHUNKS) for c in range(CHUNKS)]
    rows, place, at = [], {}, 0
    seen = [0, n_up]
    for c in range(CHUNKS):
        spans = []
        for kind, count in ((UP, ups[c]), (DOWN, downs[c])):
            spans.append((at, count * RB))
            for _ in range(count):
                place[seen[kind]] = at
                seen[kind] += 1
                at += RB
        rows.append(tuple(spans))
    return rows, place


def kernel(n_up, op_h, lift_h, src_h, tr_h, info_h, out, a, at, lf, sr, tr, st, og, lifted, hop, info, order, since,
           lsem, ssem, rsem, hsem, fsem):
    rows, place = plan(n_up)
    pos = [lax.axis_index(name) for name in AXES]
    gy, gz = pos[1], pos[2]
    odd = lax.rem(gy, 2) == 1
    high = (gz >= N // 2).astype(jnp.int32)
    ends = (gz == 3) | (gz == 4)
    ring = odd & (ends | (gz == 0) | (gz == N - 1))

    loads = [
        pltpu.make_async_copy(s, d, lsem.at[n])
        for n, (s, d) in enumerate(
            ((info_h, info), (tr_h, tr), (src_h, sr), (lift_h, lf), (op_h, a))
        )
    ]
    for load in loads:
        load.start()

    def direct(f, d):
        there = (pos[f] < N - 1) if d == UP else (pos[f] > 0)
        if f == 2:
            there &= jnp.logical_not(odd & (gz == (3 if d == UP else 4)))
        return there

    def step_to(f, d):
        return {AXES[f]: pos[f] + (1 if d == UP else -1)}

    barrier = pltpu.get_barrier_semaphore()
    peers = jnp.int32(0)
    for f in range(3):
        for d in (UP, DOWN):
            there = direct(f, d)
            peers += there.astype(jnp.int32)

            @pl.when(there)
            def _():
                pl.semaphore_signal(barrier, inc=1, device_id=step_to(f, d), device_id_type=MESH)

    peers += 2 * ring.astype(jnp.int32)
    for other in (jnp.where(ends, 0, 3), jnp.where(ends, N - 1, 4)):

        @pl.when(ring)
        def _():
            pl.semaphore_signal(barrier, inc=1, device_id={"gz": other}, device_id_type=MESH)

    for f in range(3):
        for d in (UP, DOWN):

            @pl.when(pos[f] == (0 if d == UP else N - 1))
            def _():
                for c in range(CHUNKS):
                    r0, nr = rows[c][d]
                    if nr:
                        for t in range(1, STEPS + 1):
                            st[t, r0 : r0 + nr, f * FACE : (f + 1) * FACE] = jnp.zeros((nr, FACE), BF16)

    loads[0].wait()

    def per_column(at_row):
        each = [jnp.broadcast_to(info[at_row + b : at_row + b + 1, :], (RB, 128)) for b in range(NB)]
        return jnp.concatenate(each, axis=0).astype(BF16)

    pick = jnp.where(lax.broadcasted_iota(jnp.int32, (16, 128), 1) == 0, 1.0, 0.0).astype(BF16)
    back = lax.dot_general(pick, per_column(0), NT, preferred_element_type=F32)
    rows_i = lax.broadcasted_iota(jnp.int32, (RHS, RHS), 0)
    cols_i = lax.broadcasted_iota(jnp.int32, (RHS, RHS), 1)
    before = jnp.where((rows_i >> 5) < (cols_i >> 5), 1.0, 0.0).astype(BF16)
    downs = jnp.dot(back.astype(BF16), before, preferred_element_type=F32) * (1.0 / RB)
    col = lax.broadcasted_iota(jnp.int32, (16, RHS), 1)
    key = jnp.where(back > 0.5, n_up + downs, (col >> 5).astype(F32) - downs)
    row_of = (col & (RB - 1)).astype(F32)
    for s in range(NB):
        row_of += jnp.where(key == s, float(place[s]), 0.0)
    order[...] = jnp.where(rows_i.astype(F32) == row_of[0:1, :], 1.0, 0.0).astype(BF16)
    since[...] = jnp.dot(order[...], per_column(NB), preferred_element_type=F32)
    unit = lax.broadcasted_iota(jnp.int32, (FACE, FACE), 0) == lax.broadcasted_iota(jnp.int32, (FACE, FACE), 1)
    unit = jnp.where(unit, 1.0, 0.0).astype(BF16)

    def span(f):
        return pl.ds(pl.multiple_of(f * FACE, FACE), FACE)

    loads[1].wait()
    loads[2].wait()
    loads[3].wait()
    coeffs = lax.dot_general(order[...], sr[...], NT, preferred_element_type=F32).astype(BF16)

    def begin(f, carry):
        st[0, :, span(f)] = lax.dot_general(order[...], tr[span(f), :], NT, preferred_element_type=F32).astype(BF16)
        lifted[:, span(f)] = lax.dot_general(coeffs, lf[span(f), :], NT, preferred_element_type=F32)
        return carry

    lax.fori_loop(0, 3, begin, 0)
    loads[4].wait()

    def flip(n, carry):
        k, f = n // 3, lax.rem(n, 3)
        at[span(k), span(f)] = lax.dot_general(unit, a[span(f), span(k)], NT, preferred_element_type=F32).astype(BF16)
        return carry

    lax.fori_loop(0, 9, flip, 0)

    def part(ref, t, c, d, f):
        r0, nr = rows[c][d]
        return ref.at[t, pl.ds(r0, nr), pl.ds(f * FACE, FACE)]

    def hop_part(t, c, d):
        r0, nr = rows[c][d]
        return hop.at[t, pl.ds(r0, nr), :]

    def send(t, c, d, f):
        return pltpu.make_async_remote_copy(
            src_ref=part(og, t, c, d, f), dst_ref=part(st, t + 1, c, d, f),
            send_sem=ssem.at[t, c, d, f], recv_sem=rsem.at[t, c, d, f],
            device_id=step_to(f, d), device_id_type=MESH,
        )

    def send_hop(t, c, d):
        return pltpu.make_async_remote_copy(
            src_ref=part(og, t, c, d, 2), dst_ref=hop_part(t, c, d),
            send_sem=ssem.at[t, c, d, 2], recv_sem=hsem.at[t, c],
            device_id={"gz": 0 if d == UP else N - 1}, device_id_type=MESH,
        )

    def send_on(t, c, d):
        return pltpu.make_async_remote_copy(
            src_ref=hop_part(t, c, d), dst_ref=part(st, t + 1, c, d, 2),
            send_sem=fsem.at[t, c], recv_sem=rsem.at[t, c, d, 2],
            device_id={"gz": 4 if d == UP else 3}, device_id_type=MESH,
        )

    def times(tau):
        return (tau - LAG * high, tau - LAG * (1 - high))

    def inside(t):
        return (t >= 0) & (t < STEPS)

    def arrive(t, c, d, last=STEPS - 1):
        if not rows[c][d][1]:
            return
        for f in (2, 0, 1):
            has = (pos[f] > 0) if d == UP else (pos[f] < N - 1)

            @pl.when(has & (t >= 1) & (t <= last))
            def _():
                send(t - 1, c, d, f).wait_recv()

    def sent(tau):
        for c in range(CHUNKS):
            for d, t in zip((UP, DOWN), times(tau)):
                if not rows[c][d][1]:
                    continue
                for f in range(3):
                    has = (pos[f] < N - 1) if d == UP else (pos[f] > 0)

                    @pl.when(has & inside(t - 1))
                    def _():
                        send(t - 1, c, d, f).wait_send()

                @pl.when(odd & (gz == (0 if d == UP else N - 1)) & inside(tau - 2))
                def _():
                    send_on(tau - 2, c, d).wait_send()

    def tick(tau, carry):
        ts = times(tau)
        read = [jnp.clip(t, 0, STEPS - 1) for t in ts]
        write = [jnp.clip(t, 0, STEPS) for t in ts]
        for c in range(CHUNKS):
            kinds = [d for d in (UP, DOWN) if rows[c][d][1]]
            for d in kinds:
                arrive(ts[d], c, d)

            def face(n, carry):
                f = lax.rem(n + 2, 3)
                x = jnp.concatenate([st[read[d], rows[c][d][0] : sum(rows[c][d]), :] for d in kinds], axis=0)
                acc = jnp.dot(x, at[:, span(f)], preferred_element_type=F32)
                at_row = 0
                for d in kinds:
                    r0, nr = rows[c][d]
                    gate = jnp.where(since[r0 : r0 + nr, :] <= ts[d].astype(F32), 1.0, 0.0)
                    gate = jnp.concatenate([gate] * (FACE // 128), axis=1)
                    total = acc[at_row : at_row + nr] + gate * lifted[r0 : r0 + nr, span(f)]
                    og[write[d], r0 : r0 + nr, span(f)] = total.astype(BF16)
                    at_row += nr
                for d in kinds:
                    for g in range(3):

                        @pl.when((f == g) & direct(g, d) & inside(ts[d]))
                        def _():
                            send(ts[d], c, d, g).start()

                    @pl.when((f == 2) & odd & (gz == (3 if d == UP else 4)) & inside(ts[d]))
                    def _():
                        send_hop(ts[d], c, d).start()

                return carry

            lax.fori_loop(0, 3, face, 0)
            for d in kinds:

                @pl.when(odd & (gz == (0 if d == UP else N - 1)) & inside(tau - 1))
                def _():
                    send_hop(tau - 1, c, d).wait_recv()
                    send_on(tau - 1, c, d).start()

        sent(tau)
        return carry

    pl.semaphore_wait(barrier, peers)
    lax.fori_loop(0, STEPS + LAG, tick, 0)
    sent(jnp.int32(STEPS + LAG))
    for c in range(CHUNKS):
        for d in (UP, DOWN):
            arrive(jnp.int32(STEPS), c, d, STEPS)

    def finish(f, carry):
        block = lax.dot_general(unit, st[STEPS, :, span(f)], NT, preferred_element_type=F32).astype(BF16)
        out[span(f), :] = jnp.dot(block, order[...], preferred_element_type=F32).astype(BF16)
        return carry

    lax.fori_loop(0, 3, finish, 0)


def sweep(n_up, operator, lift, source, traces_in, info):
    anywhere = pl.BlockSpec(memory_space=pl.ANY)
    return pl.pallas_call(
        functools.partial(kernel, n_up),
        out_shape=jax.ShapeDtypeStruct((ORDER, RHS), BF16),
        in_specs=[anywhere] * 5,
        out_specs=pl.BlockSpec(memory_space=pltpu.VMEM),
        scratch_shapes=[
            pltpu.VMEM((ORDER, ORDER), BF16),
            pltpu.VMEM((ORDER, ORDER), BF16),
            pltpu.VMEM((ORDER, SRC), BF16),
            pltpu.VMEM((SRC, RHS), BF16),
            pltpu.VMEM((ORDER, RHS), BF16),
            pltpu.VMEM((STEPS + 1, RHS, ORDER), BF16),
            pltpu.VMEM((STEPS + 1, RHS, ORDER), BF16),
            pltpu.VMEM((RHS, ORDER), F32),
            pltpu.VMEM((STEPS, RHS, FACE), BF16),
            pltpu.VMEM((16, 128), F32),
            pltpu.VMEM((RHS, RHS), BF16),
            pltpu.VMEM((RHS, 128), F32),
            pltpu.SemaphoreType.DMA((5,)),
            pltpu.SemaphoreType.DMA((STEPS, CHUNKS, 2, 3)),
            pltpu.SemaphoreType.DMA((STEPS, CHUNKS, 2, 3)),
            pltpu.SemaphoreType.DMA((STEPS, CHUNKS)),
            pltpu.SemaphoreType.DMA((STEPS, CHUNKS)),
        ],
        compiler_params=pltpu.CompilerParams(
            collective_id=n_up, has_side_effects=True, vmem_limit_bytes=40 * 2**20
        ),
        name=f"sweep_{n_up}",
    )(operator, lift, source, traces_in, info)


VARIANTS = tuple(range(NB + 1))


def body(operator, lift, source, traces_in, depth, direction):
    info = jnp.broadcast_to(jnp.concatenate([direction, depth]).astype(F32)[:, None], (2 * NB, 128))
    args = (operator[0, 0, 0], lift[0, 0, 0], source[0, 0, 0], traces_in[0, 0, 0], info)
    n_up = NB - jnp.sum((direction == 1).astype(jnp.int32))
    result = lax.switch(n_up, [functools.partial(sweep, n) for n in VARIANTS], *args)
    return result[None, None, None]


def solution(mesh):
    placed = (
        P("gx", "gy", "gz", None, None),
        P("gx", "gy", "gz", None, None),
        P("gx", "gy", "gz", None, None),
        P("gx", "gy", "gz", None, None),
        P(),
        P(),
    )
    return jax.shard_map(
        body, mesh=mesh, in_specs=placed, out_specs=P("gx", "gy", "gz", None, None), check_vma=False
    )
```

```python
import functools

import jax
import jax.numpy as jnp
from jax import lax
from jax.experimental import pallas as pl
from jax.experimental.pallas import tpu as pltpu
from jax.sharding import PartitionSpec as P

MESH = pl.DeviceIdType.MESH
FACE = 384
ORDER = 1152
SRC = 128
NB = 8
RB = 32
RHS = NB * RB
STEPS = 6
N = 8
CHUNKS = 2
LAG = 1
UNROLL = (2, 6)
UP, DOWN = 0, 1
AXES = ("gx", "gy", "gz")
F32, BF16 = jnp.float32, jnp.bfloat16
NT = (((1,), (1,)), ((), ()))


def plan(n_up):
    ups = [n_up // CHUNKS + (c < n_up % CHUNKS) for c in range(CHUNKS)]
    n_down = NB - n_up
    downs = [n_down // CHUNKS + (CHUNKS - 1 - c < n_down % CHUNKS) for c in range(CHUNKS)]
    rows, place, at = [], {}, 0
    seen = [0, n_up]
    for c in range(CHUNKS):
        spans = []
        for kind, count in ((UP, ups[c]), (DOWN, downs[c])):
            spans.append((at, count * RB))
            for _ in range(count):
                place[seen[kind]] = at
                seen[kind] += 1
                at += RB
        rows.append(tuple(spans))
    return rows, place


def kernel(n_up, op_h, lift_h, src_h, tr_h, info_h, out, a, at, lf, sr, tr, st, og, lifted, hop, info, order, since,
           lsem, ssem, rsem, hsem, fsem):
    rows, place = plan(n_up)
    pos = [lax.axis_index(name) for name in AXES]
    gy, gz = pos[1], pos[2]
    odd = lax.rem(gy, 2) == 1
    high = (gz >= N // 2).astype(jnp.int32)
    ends = (gz == 3) | (gz == 4)
    ring = odd & (ends | (gz == 0) | (gz == N - 1))

    loads = [
        pltpu.make_async_copy(s, d, lsem.at[n])
        for n, (s, d) in enumerate(
            ((info_h, info), (tr_h, tr), (src_h, sr), (lift_h, lf), (op_h, a))
        )
    ]
    for load in loads:
        load.start()

    def direct(f, d):
        there = (pos[f] < N - 1) if d == UP else (pos[f] > 0)
        if f == 2:
            there &= jnp.logical_not(odd & (gz == (3 if d == UP else 4)))
        return there

    def step_to(f, d):
        return {AXES[f]: pos[f] + (1 if d == UP else -1)}

    barrier = pltpu.get_barrier_semaphore()
    peers = jnp.int32(0)
    for f in range(3):
        for d in (UP, DOWN):
            there = direct(f, d)
            peers += there.astype(jnp.int32)

            @pl.when(there)
            def _():
                pl.semaphore_signal(barrier, inc=1, device_id=step_to(f, d), device_id_type=MESH)

    peers += 2 * ring.astype(jnp.int32)
    for other in (jnp.where(ends, 0, 3), jnp.where(ends, N - 1, 4)):

        @pl.when(ring)
        def _():
            pl.semaphore_signal(barrier, inc=1, device_id={"gz": other}, device_id_type=MESH)

    for f in range(3):
        for d in (UP, DOWN):

            @pl.when(pos[f] == (0 if d == UP else N - 1))
            def _():
                for c in range(CHUNKS):
                    r0, nr = rows[c][d]
                    if nr:
                        for t in range(1, STEPS + 1):
                            st[t, r0 : r0 + nr, f * FACE : (f + 1) * FACE] = jnp.zeros((nr, FACE), BF16)

    loads[0].wait()

    def per_column(at_row):
        each = [jnp.broadcast_to(info[at_row + b : at_row + b + 1, :], (RB, 128)) for b in range(NB)]
        return jnp.concatenate(each, axis=0).astype(BF16)

    pick = jnp.where(lax.broadcasted_iota(jnp.int32, (16, 128), 1) == 0, 1.0, 0.0).astype(BF16)
    back = lax.dot_general(pick, per_column(0), NT, preferred_element_type=F32)
    rows_i = lax.broadcasted_iota(jnp.int32, (RHS, RHS), 0)
    cols_i = lax.broadcasted_iota(jnp.int32, (RHS, RHS), 1)
    before = jnp.where((rows_i >> 5) < (cols_i >> 5), 1.0, 0.0).astype(BF16)
    downs = jnp.dot(back.astype(BF16), before, preferred_element_type=F32) * (1.0 / RB)
    col = lax.broadcasted_iota(jnp.int32, (16, RHS), 1)
    key = jnp.where(back > 0.5, n_up + downs, (col >> 5).astype(F32) - downs)
    row_of = (col & (RB - 1)).astype(F32)
    for s in range(NB):
        row_of += jnp.where(key == s, float(place[s]), 0.0)
    order[...] = jnp.where(rows_i.astype(F32) == row_of[0:1, :], 1.0, 0.0).astype(BF16)
    since[...] = jnp.dot(order[...], per_column(NB), preferred_element_type=F32)
    unit = lax.broadcasted_iota(jnp.int32, (FACE, FACE), 0) == lax.broadcasted_iota(jnp.int32, (FACE, FACE), 1)
    unit = jnp.where(unit, 1.0, 0.0).astype(BF16)

    def span(f):
        if isinstance(f, int):
            return slice(f * FACE, (f + 1) * FACE)
        return pl.ds(pl.multiple_of(f * FACE, FACE), FACE)

    loads[1].wait()
    loads[2].wait()
    loads[3].wait()
    coeffs = lax.dot_general(order[...], sr[...], NT, preferred_element_type=F32).astype(BF16)

    def begin(f, carry):
        st[0, :, span(f)] = lax.dot_general(order[...], tr[span(f), :], NT, preferred_element_type=F32).astype(BF16)
        lifted[:, span(f)] = lax.dot_general(coeffs, lf[span(f), :], NT, preferred_element_type=F32)
        return carry

    lax.fori_loop(0, 3, begin, 0)
    loads[4].wait()

    def flip(n, carry):
        k, f = n // 3, lax.rem(n, 3)
        at[span(k), span(f)] = lax.dot_general(unit, a[span(f), span(k)], NT, preferred_element_type=F32).astype(BF16)
        return carry

    def part(ref, t, c, d, f):
        r0, nr = rows[c][d]
        return ref.at[t, pl.ds(r0, nr), pl.ds(f * FACE, FACE)]

    def hop_part(t, c, d):
        r0, nr = rows[c][d]
        return hop.at[t, pl.ds(r0, nr), :]

    def send(t, c, d, f):
        return pltpu.make_async_remote_copy(
            src_ref=part(og, t, c, d, f), dst_ref=part(st, t + 1, c, d, f),
            send_sem=ssem.at[t, c, d, f], recv_sem=rsem.at[t, c, d, f],
            device_id=step_to(f, d), device_id_type=MESH,
        )

    def send_hop(t, c, d):
        return pltpu.make_async_remote_copy(
            src_ref=part(og, t, c, d, 2), dst_ref=hop_part(t, c, d),
            send_sem=ssem.at[t, c, d, 2], recv_sem=hsem.at[t, c],
            device_id={"gz": 0 if d == UP else N - 1}, device_id_type=MESH,
        )

    def send_on(t, c, d):
        return pltpu.make_async_remote_copy(
            src_ref=hop_part(t, c, d), dst_ref=part(st, t + 1, c, d, 2),
            send_sem=fsem.at[t, c], recv_sem=rsem.at[t, c, d, 2],
            device_id={"gz": 4 if d == UP else 3}, device_id_type=MESH,
        )

    def times(tau):
        return (tau - LAG * high, tau - LAG * (1 - high))

    def inside(t):
        return (t >= 0) & (t < STEPS)

    def arrive(t, c, d, last=STEPS - 1):
        if not rows[c][d][1]:
            return
        for f in (2, 0, 1):
            has = (pos[f] > 0) if d == UP else (pos[f] < N - 1)

            @pl.when(has & (t >= 1) & (t <= last))
            def _():
                send(t - 1, c, d, f).wait_recv()

    def sent(tau):
        for c in range(CHUNKS):
            for d, t in zip((UP, DOWN), times(tau)):
                if not rows[c][d][1]:
                    continue
                for f in range(3):
                    has = (pos[f] < N - 1) if d == UP else (pos[f] > 0)

                    @pl.when(has & inside(t - 1))
                    def _():
                        send(t - 1, c, d, f).wait_send()

                @pl.when(odd & (gz == (0 if d == UP else N - 1)) & inside(tau - 2))
                def _():
                    send_on(tau - 2, c, d).wait_send()

    def tick(tau, first, unroll):
        ts = times(tau)
        read = [jnp.clip(t, 0, STEPS - 1) for t in ts]
        write = [jnp.clip(t, 0, STEPS) for t in ts]
        for c in range(CHUNKS):
            kinds = [d for d in (UP, DOWN) if rows[c][d][1]]
            if not first:
                for d in kinds:

                    @pl.when(odd & (gz == (0 if d == UP else N - 1)) & inside(tau - 1))
                    def _():
                        send_hop(tau - 1, c, d).wait_recv()
                        send_on(tau - 1, c, d).start()

                for d in kinds:
                    arrive(ts[d], c, d)

            def face(f):
                x = jnp.concatenate([st[read[d], rows[c][d][0] : sum(rows[c][d]), :] for d in kinds], axis=0)
                if first:
                    acc = lax.dot_general(x, a[span(f), :], NT, preferred_element_type=F32)
                else:
                    acc = jnp.dot(x, at[:, span(f)], preferred_element_type=F32)
                at_row = 0
                for d in kinds:
                    r0, nr = rows[c][d]
                    gate = jnp.where(since[r0 : r0 + nr, :] <= ts[d].astype(F32), 1.0, 0.0)
                    gate = jnp.concatenate([gate] * (FACE // 128), axis=1)
                    total = acc[at_row : at_row + nr] + gate * lifted[r0 : r0 + nr, span(f)]
                    og[write[d], r0 : r0 + nr, span(f)] = total.astype(BF16)
                    at_row += nr
                for d in kinds:
                    for g in range(3):
                        if unroll and f != g:
                            continue
                        go = direct(g, d) & inside(ts[d])

                        @pl.when(go if unroll else go & (f == g))
                        def _():
                            send(ts[d], c, d, g).start()

                    if unroll and f != 2:
                        continue
                    go = odd & (gz == (3 if d == UP else 4)) & inside(ts[d])

                    @pl.when(go if unroll else go & (f == 2))
                    def _():
                        send_hop(ts[d], c, d).start()

            if unroll:
                for f in (2, 0, 1):
                    face(f)
            else:

                def turn(n, carry):
                    face(lax.rem(n + 2, 3))
                    return carry

                lax.fori_loop(0, 3, turn, 0)

        if not first:
            sent(tau)

    def main(tau, carry):
        tick(tau, False, UNROLL[0] <= n_up <= UNROLL[1])
        return carry

    pl.semaphore_wait(barrier, peers)
    tick(jnp.int32(0), True, False)
    lax.fori_loop(0, 9, flip, 0)
    lax.fori_loop(1, STEPS + LAG, main, 0)
    sent(jnp.int32(STEPS + LAG))
    for c in range(CHUNKS):
        for d in (UP, DOWN):
            arrive(jnp.int32(STEPS), c, d, STEPS)

    def finish(f, carry):
        block = lax.dot_general(unit, st[STEPS, :, span(f)], NT, preferred_element_type=F32).astype(BF16)
        out[span(f), :] = jnp.dot(block, order[...], preferred_element_type=F32).astype(BF16)
        return carry

    lax.fori_loop(0, 3, finish, 0)


def sweep(n_up, operator, lift, source, traces_in, info):
    anywhere = pl.BlockSpec(memory_space=pl.ANY)
    return pl.pallas_call(
        functools.partial(kernel, n_up),
        out_shape=jax.ShapeDtypeStruct((ORDER, RHS), BF16),
        in_specs=[anywhere] * 5,
        out_specs=pl.BlockSpec(memory_space=pltpu.VMEM),
        scratch_shapes=[
            pltpu.VMEM((ORDER, ORDER), BF16),
            pltpu.VMEM((ORDER, ORDER), BF16),
            pltpu.VMEM((ORDER, SRC), BF16),
            pltpu.VMEM((SRC, RHS), BF16),
            pltpu.VMEM((ORDER, RHS), BF16),
            pltpu.VMEM((STEPS + 1, RHS, ORDER), BF16),
            pltpu.VMEM((STEPS + 1, RHS, ORDER), BF16),
            pltpu.VMEM((RHS, ORDER), F32),
            pltpu.VMEM((STEPS, RHS, FACE), BF16),
            pltpu.VMEM((16, 128), F32),
            pltpu.VMEM((RHS, RHS), BF16),
            pltpu.VMEM((RHS, 128), F32),
            pltpu.SemaphoreType.DMA((5,)),
            pltpu.SemaphoreType.DMA((STEPS, CHUNKS, 2, 3)),
            pltpu.SemaphoreType.DMA((STEPS, CHUNKS, 2, 3)),
            pltpu.SemaphoreType.DMA((STEPS, CHUNKS)),
            pltpu.SemaphoreType.DMA((STEPS, CHUNKS)),
        ],
        compiler_params=pltpu.CompilerParams(
            collective_id=n_up, has_side_effects=True, vmem_limit_bytes=40 * 2**20
        ),
        name=f"sweep_{n_up}",
    )(operator, lift, source, traces_in, info)


VARIANTS = tuple(range(NB + 1))


def body(operator, lift, source, traces_in, depth, direction):
    info = jnp.broadcast_to(jnp.concatenate([direction, depth]).astype(F32)[:, None], (2 * NB, 128))
    args = (operator[0, 0, 0], lift[0, 0, 0], source[0, 0, 0], traces_in[0, 0, 0], info)
    n_up = NB - jnp.sum((direction == 1).astype(jnp.int32))
    result = lax.switch(n_up, [functools.partial(sweep, n) for n in VARIANTS], *args)
    return result[None, None, None]


def solution(mesh):
    placed = (
        P("gx", "gy", "gz", None, None),
        P("gx", "gy", "gz", None, None),
        P("gx", "gy", "gz", None, None),
        P("gx", "gy", "gz", None, None),
        P(),
        P(),
    )
    return jax.shard_map(
        body, mesh=mesh, in_specs=placed, out_specs=P("gx", "gy", "gz", None, None), check_vma=False
    )
```

```python
import functools

import jax
import jax.numpy as jnp
from jax import lax
from jax.experimental import pallas as pl
from jax.experimental.pallas import tpu as pltpu
from jax.sharding import PartitionSpec as P

MESH = pl.DeviceIdType.MESH
FACE = 384
ORDER = 1152
SRC = 128
NB = 8
RB = 32
RHS = NB * RB
STEPS = 6
N = 8
CHUNKS = 2
LAG = 1
UNROLL = (2, 6)
UP, DOWN = 0, 1
AXES = ("gx", "gy", "gz")
F32, BF16 = jnp.float32, jnp.bfloat16
NT = (((1,), (1,)), ((), ()))


def plan(n_up):
    ups = [n_up // CHUNKS + (c < n_up % CHUNKS) for c in range(CHUNKS)]
    n_down = NB - n_up
    downs = [n_down // CHUNKS + (CHUNKS - 1 - c < n_down % CHUNKS) for c in range(CHUNKS)]
    rows, place, at = [], {}, 0
    seen = [0, n_up]
    for c in range(CHUNKS):
        spans = []
        for kind, count in ((UP, ups[c]), (DOWN, downs[c])):
            spans.append((at, count * RB))
            for _ in range(count):
                place[seen[kind]] = at
                seen[kind] += 1
                at += RB
        rows.append(tuple(spans))
    return rows, place


def kernel(n_up, op_h, lift_h, src_h, tr_h, info_h, out, a, at, lf, sr, tr, st, og, lifted, hop, info, order, since,
           lsem, ssem, rsem, hsem, fsem):
    rows, place = plan(n_up)
    pos = [lax.axis_index(name) for name in AXES]
    gy, gz = pos[1], pos[2]
    odd = lax.rem(gy, 2) == 1
    high = (gz >= N // 2).astype(jnp.int32)
    ends = (gz == 3) | (gz == 4)
    ring = odd & (ends | (gz == 0) | (gz == N - 1))

    loads = [
        pltpu.make_async_copy(s, d, lsem.at[n])
        for n, (s, d) in enumerate(
            ((info_h, info), (tr_h, tr), (src_h, sr), (lift_h, lf), (op_h, a))
        )
    ]
    for load in loads:
        load.start()

    def direct(f, d):
        there = (pos[f] < N - 1) if d == UP else (pos[f] > 0)
        if f == 2:
            there &= jnp.logical_not(odd & (gz == (3 if d == UP else 4)))
        return there

    def step_to(f, d):
        return {AXES[f]: pos[f] + (1 if d == UP else -1)}

    barrier = pltpu.get_barrier_semaphore()
    peers = jnp.int32(0)
    for f in range(3):
        for d in (UP, DOWN):
            there = direct(f, d)
            peers += there.astype(jnp.int32)

            @pl.when(there)
            def _():
                pl.semaphore_signal(barrier, inc=1, device_id=step_to(f, d), device_id_type=MESH)

    peers += 2 * ring.astype(jnp.int32)
    for other in (jnp.where(ends, 0, 3), jnp.where(ends, N - 1, 4)):

        @pl.when(ring)
        def _():
            pl.semaphore_signal(barrier, inc=1, device_id={"gz": other}, device_id_type=MESH)

    for f in range(3):
        for d in (UP, DOWN):

            @pl.when(pos[f] == (0 if d == UP else N - 1))
            def _():
                for c in range(CHUNKS):
                    r0, nr = rows[c][d]
                    if nr:
                        for t in range(1, STEPS + 1):
                            st[t, r0 : r0 + nr, f * FACE : (f + 1) * FACE] = jnp.zeros((nr, FACE), BF16)

    loads[0].wait()

    def per_column(at_row):
        each = [jnp.broadcast_to(info[at_row + b : at_row + b + 1, :], (RB, 128)) for b in range(NB)]
        return jnp.concatenate(each, axis=0).astype(BF16)

    pick = jnp.where(lax.broadcasted_iota(jnp.int32, (16, 128), 1) == 0, 1.0, 0.0).astype(BF16)
    back = lax.dot_general(pick, per_column(0), NT, preferred_element_type=F32)
    rows_i = lax.broadcasted_iota(jnp.int32, (RHS, RHS), 0)
    cols_i = lax.broadcasted_iota(jnp.int32, (RHS, RHS), 1)
    before = jnp.where((rows_i >> 5) < (cols_i >> 5), 1.0, 0.0).astype(BF16)
    downs = jnp.dot(back.astype(BF16), before, preferred_element_type=F32) * (1.0 / RB)
    col = lax.broadcasted_iota(jnp.int32, (16, RHS), 1)
    key = jnp.where(back > 0.5, n_up + downs, (col >> 5).astype(F32) - downs)
    row_of = (col & (RB - 1)).astype(F32)
    for s in range(NB):
        row_of += jnp.where(key == s, float(place[s]), 0.0)
    order[...] = jnp.where(rows_i.astype(F32) == row_of[0:1, :], 1.0, 0.0).astype(BF16)
    since[...] = jnp.dot(order[...], per_column(NB), preferred_element_type=F32)
    unit = lax.broadcasted_iota(jnp.int32, (FACE, FACE), 0) == lax.broadcasted_iota(jnp.int32, (FACE, FACE), 1)
    unit = jnp.where(unit, 1.0, 0.0).astype(BF16)

    def span(f):
        if isinstance(f, int):
            return slice(f * FACE, (f + 1) * FACE)
        return pl.ds(pl.multiple_of(f * FACE, FACE), FACE)

    loads[1].wait()
    loads[2].wait()
    loads[3].wait()
    coeffs = lax.dot_general(order[...], sr[...], NT, preferred_element_type=F32).astype(BF16)

    def begin(f, carry):
        st[0, :, span(f)] = lax.dot_general(order[...], tr[span(f), :], NT, preferred_element_type=F32).astype(BF16)
        lifted[:, span(f)] = lax.dot_general(coeffs, lf[span(f), :], NT, preferred_element_type=F32)
        return carry

    lax.fori_loop(0, 3, begin, 0)
    loads[4].wait()

    def flip(n, carry):
        k, f = n // 3, lax.rem(n, 3)
        at[span(k), span(lax.rem(f + 1, 3))] = lax.dot_general(unit, a[span(f), span(k)], NT, preferred_element_type=F32).astype(BF16)
        return carry

    def part(ref, t, c, d, f):
        r0, nr = rows[c][d]
        return ref.at[t, pl.ds(r0, nr), pl.ds(f * FACE, FACE)]

    def hop_part(t, c, d):
        r0, nr = rows[c][d]
        return hop.at[t, pl.ds(r0, nr), :]

    def send(t, c, d, f):
        return pltpu.make_async_remote_copy(
            src_ref=part(og, t, c, d, f), dst_ref=part(st, t + 1, c, d, f),
            send_sem=ssem.at[t, c, d, f], recv_sem=rsem.at[t, c, d, f],
            device_id=step_to(f, d), device_id_type=MESH,
        )

    def send_hop(t, c, d):
        return pltpu.make_async_remote_copy(
            src_ref=part(og, t, c, d, 2), dst_ref=hop_part(t, c, d),
            send_sem=ssem.at[t, c, d, 2], recv_sem=hsem.at[t, c],
            device_id={"gz": 0 if d == UP else N - 1}, device_id_type=MESH,
        )

    def send_on(t, c, d):
        return pltpu.make_async_remote_copy(
            src_ref=hop_part(t, c, d), dst_ref=part(st, t + 1, c, d, 2),
            send_sem=fsem.at[t, c], recv_sem=rsem.at[t, c, d, 2],
            device_id={"gz": 4 if d == UP else 3}, device_id_type=MESH,
        )

    def times(tau):
        return (tau - LAG * high, tau - LAG * (1 - high))

    def inside(t):
        return (t >= 0) & (t < STEPS)

    def arrive(t, c, d, last=STEPS - 1):
        if not rows[c][d][1]:
            return
        for f in (2, 0, 1):
            has = (pos[f] > 0) if d == UP else (pos[f] < N - 1)

            @pl.when(has & (t >= 1) & (t <= last))
            def _():
                send(t - 1, c, d, f).wait_recv()

    def sent(tau):
        for c in range(CHUNKS):
            for d, t in zip((UP, DOWN), times(tau)):
                if not rows[c][d][1]:
                    continue
                for f in range(3):
                    has = (pos[f] < N - 1) if d == UP else (pos[f] > 0)

                    @pl.when(has & inside(t - 1))
                    def _():
                        send(t - 1, c, d, f).wait_send()

                @pl.when(odd & (gz == (0 if d == UP else N - 1)) & inside(tau - 2))
                def _():
                    send_on(tau - 2, c, d).wait_send()

    def tick(tau, first, unroll):
        ts = times(tau)
        read = [jnp.clip(t, 0, STEPS - 1) for t in ts]
        write = [jnp.clip(t, 0, STEPS) for t in ts]
        for c in range(CHUNKS):
            kinds = [d for d in (UP, DOWN) if rows[c][d][1]]
            if not first:
                for d in kinds:

                    @pl.when(odd & (gz == (0 if d == UP else N - 1)) & inside(tau - 1))
                    def _():
                        send_hop(tau - 1, c, d).wait_recv()
                        send_on(tau - 1, c, d).start()

                for d in kinds:
                    arrive(ts[d], c, d)

            def state():
                return jnp.concatenate([st[read[d], rows[c][d][0] : sum(rows[c][d]), :] for d in kinds], axis=0)

            def multiply(x, place_of, count):
                lanes = span(place_of) if count == 1 else slice(0, count * FACE)
                return jnp.dot(x, at[:, lanes], preferred_element_type=F32)

            def face(f, acc=None):
                x = state()
                if first:
                    acc = lax.dot_general(x, a[span(f), :], NT, preferred_element_type=F32)
                elif acc is None:
                    acc = multiply(x, (f + 1) % 3 if unroll else lax.rem(f + 1, 3), 1)
                at_row = 0
                for d in kinds:
                    r0, nr = rows[c][d]
                    gate = jnp.where(since[r0 : r0 + nr, :] <= ts[d].astype(F32), 1.0, 0.0)
                    gate = jnp.concatenate([gate] * (FACE // 128), axis=1)
                    total = acc[at_row : at_row + nr] + gate * lifted[r0 : r0 + nr, span(f)]
                    og[write[d], r0 : r0 + nr, span(f)] = total.astype(BF16)
                    at_row += nr
                for d in kinds:
                    for g in range(3):
                        if unroll and f != g:
                            continue
                        go = direct(g, d) & inside(ts[d])

                        @pl.when(go if unroll else go & (f == g))
                        def _():
                            send(ts[d], c, d, g).start()

                    if unroll and f != 2:
                        continue
                    go = odd & (gz == (3 if d == UP else 4)) & inside(ts[d])

                    @pl.when(go if unroll else go & (f == 2))
                    def _():
                        send_hop(ts[d], c, d).start()

            if unroll:
                both = multiply(state(), 0, 2)
                face(2, both[:, :FACE])
                face(0, both[:, FACE:])
                face(1)
            else:

                def turn(n, carry):
                    face(lax.rem(n + 2, 3))
                    return carry

                lax.fori_loop(0, 3, turn, 0)

        if not first:
            sent(tau)

    def main(tau, carry):
        tick(tau, False, UNROLL[0] <= n_up <= UNROLL[1])
        return carry

    pl.semaphore_wait(barrier, peers)
    tick(jnp.int32(0), True, False)
    lax.fori_loop(0, 9, flip, 0)
    lax.fori_loop(1, STEPS + LAG, main, 0)
    sent(jnp.int32(STEPS + LAG))
    for c in range(CHUNKS):
        for d in (UP, DOWN):
            arrive(jnp.int32(STEPS), c, d, STEPS)

    def finish(f, carry):
        block = lax.dot_general(unit, st[STEPS, :, span(f)], NT, preferred_element_type=F32).astype(BF16)
        out[span(f), :] = jnp.dot(block, order[...], preferred_element_type=F32).astype(BF16)
        return carry

    lax.fori_loop(0, 3, finish, 0)


def sweep(n_up, operator, lift, source, traces_in, info):
    anywhere = pl.BlockSpec(memory_space=pl.ANY)
    return pl.pallas_call(
        functools.partial(kernel, n_up),
        out_shape=jax.ShapeDtypeStruct((ORDER, RHS), BF16),
        in_specs=[anywhere] * 5,
        out_specs=pl.BlockSpec(memory_space=pltpu.VMEM),
        scratch_shapes=[
            pltpu.VMEM((ORDER, ORDER), BF16),
            pltpu.VMEM((ORDER, ORDER), BF16),
            pltpu.VMEM((ORDER, SRC), BF16),
            pltpu.VMEM((SRC, RHS), BF16),
            pltpu.VMEM((ORDER, RHS), BF16),
            pltpu.VMEM((STEPS + 1, RHS, ORDER), BF16),
            pltpu.VMEM((STEPS + 1, RHS, ORDER), BF16),
            pltpu.VMEM((RHS, ORDER), F32),
            pltpu.VMEM((STEPS, RHS, FACE), BF16),
            pltpu.VMEM((16, 128), F32),
            pltpu.VMEM((RHS, RHS), BF16),
            pltpu.VMEM((RHS, 128), F32),
            pltpu.SemaphoreType.DMA((5,)),
            pltpu.SemaphoreType.DMA((STEPS, CHUNKS, 2, 3)),
            pltpu.SemaphoreType.DMA((STEPS, CHUNKS, 2, 3)),
            pltpu.SemaphoreType.DMA((STEPS, CHUNKS)),
            pltpu.SemaphoreType.DMA((STEPS, CHUNKS)),
        ],
        compiler_params=pltpu.CompilerParams(
            collective_id=n_up, has_side_effects=True, vmem_limit_bytes=40 * 2**20
        ),
        name=f"sweep_{n_up}",
    )(operator, lift, source, traces_in, info)


VARIANTS = tuple(range(NB + 1))


def body(operator, lift, source, traces_in, depth, direction):
    info = jnp.broadcast_to(jnp.concatenate([direction, depth]).astype(F32)[:, None], (2 * NB, 128))
    args = (operator[0, 0, 0], lift[0, 0, 0], source[0, 0, 0], traces_in[0, 0, 0], info)
    n_up = NB - jnp.sum((direction == 1).astype(jnp.int32))
    result = lax.switch(n_up, [functools.partial(sweep, n) for n in VARIANTS], *args)
    return result[None, None, None]


def solution(mesh):
    placed = (
        P("gx", "gy", "gz", None, None),
        P("gx", "gy", "gz", None, None),
        P("gx", "gy", "gz", None, None),
        P("gx", "gy", "gz", None, None),
        P(),
        P(),
    )
    return jax.shard_map(
        body, mesh=mesh, in_specs=placed, out_specs=P("gx", "gy", "gz", None, None), check_vma=False
    )
```
